32 devices in a mesh: px: 8 (over y, x, core), py: 4 (over z).
Axes of the slice: x: 2, y: 2, z: 4, core: 2. Of those that a mesh axis runs over, the one named last changes fastest.
Arguments:
- displacement: float32 [60, 16, 8, 128], P(None, 'px', 'py'), may hold values from -4 to 4
- velocity: float32 [60, 16, 8, 128], P(None, 'px', 'py'), may hold values from -6 to 6
- modulus: float32 [16, 8, 128], P('px', 'py'), may hold values from 0.5 to 4
- gradient_map: float32 [243, 60], replicated, may hold values from -0.75 to 0.75
- trace_map: float32 [6, 54, 60], replicated, may hold values from -0.75 to 0.75
- lift_map: float32 [6, 60, 54], replicated, may hold values from -0.3125 to 0.3125
- split_map: float32 [27, 27], replicated, may hold values from -1.25 to 1.25
- spread_map: float32 [6, 60, 27], replicated, may hold values from -1.25 to 1.25
- fracture_faces: int32 [32, 512], P(('px', 'py')), may hold values from 0 to 1534, as said below
- fracture_counts: int32 [32, 3], P(('px', 'py')), may hold values from 0 to 256, as said below
Outputs:
- displacement_out: float32 [60, 16, 8, 128], P(None, 'px', 'py')
- velocity_out: float32 [60, 16, 8, 128], P(None, 'px', 'py')
The draws below stay inside these ranges and needn't reach their ends.
Inputs may be any that keep to these rules, and one draw needn't show every extreme that they name: `fracture_faces`: row p holds the device at index p of px+py (px major). With local element numbers (i * 2 + j) * 128 + k and face ids d * 2 * 2 * 128 + element, slots 0 to 127 name +x faces of elements with i = 1, the next 128 slots +y faces of elements with j = 1, the last 256 slots faces whose neighbour lies on the same device. All ids of a row differ. Only the first fracture_counts[p, s] slots of section s open. `fracture_counts`: counts of opened slots in the three sections of a row. The first is 0 on devices with the last px index, the second on devices with the last py index; over all devices the sections reach 128, 128 and 256.
All inputs are finite; a program needn't handle non-finite values.
Results may differ from the reference program's by a relative error of at most 0.0003.
Values sent between devices are 32-bit elements; how exact they have to be, the bound alone decides.
A program may use at most 64 MiB of HBM per device.

```python
import math
import jax
import jax.numpy as jnp
from jax import lax

QUAD = 27
FACE_QUAD = 9
DOF = 60
CX = 2
CY = 2
EZ = 128
BLK_CAP = 128
LOC_CAP = 256
NX = 16
NY = 8
N_PX = 8
N_PY = 4
DEVICES = 32


def fracture_plan(key):
    base_key = jax.random.fold_in(key, 7)
    keys = jax.random.split(base_key, 9)
    device = jnp.arange(DEVICES, dtype=jnp.int32)
    device_x = device // N_PY
    device_y = device % N_PY
    x_raw = jax.random.randint(keys[0], (DEVICES,), 0, BLK_CAP + 1)
    x_full = jax.random.randint(keys[1], (), 0, (N_PX - 1) * N_PY)
    x_count = jnp.where(device == x_full, BLK_CAP, x_raw)
    x_count = jnp.where(device_x < N_PX - 1, x_count, 0)
    y_raw = jax.random.randint(keys[2], (DEVICES,), 0, BLK_CAP + 1)
    y_full = jax.random.randint(keys[3], (), 0, N_PX) * N_PY + jax.random.randint(keys[4], (), 0, N_PY - 1)
    y_count = jnp.where(device == y_full, BLK_CAP, y_raw)
    y_count = jnp.where(device_y < N_PY - 1, y_count, 0)
    first_draw = jax.random.randint(keys[5], (DEVICES,), 0, LOC_CAP + 1)
    second_draw = jax.random.randint(keys[6], (DEVICES,), 0, LOC_CAP + 1)
    local_count = first_draw * second_draw // LOC_CAP
    local_full = jax.random.randint(keys[7], (), 0, DEVICES)
    local_count = jnp.where(device == local_full, LOC_CAP, local_count)
    counts = jnp.stack([x_count, y_count, local_count], axis=1).astype(jnp.int32)
    elements = CX * CY * EZ
    device_keys = jax.random.split(keys[8], DEVICES)

    def one_device(device_key):
        key_x, key_y, key_local = jax.random.split(device_key, 3)
        spot_x = jax.random.permutation(key_x, CY * EZ)[:BLK_CAP]
        x_ids = (CX - 1) * CY * EZ + spot_x
        spot_y = jax.random.permutation(key_y, CX * EZ)[:BLK_CAP]
        y_ids = elements + (spot_y // EZ * CY + CY - 1) * EZ + spot_y % EZ
        candidate = jnp.arange(3 * elements, dtype=jnp.int32)
        direction = candidate // elements
        element = candidate % elements
        inner_face = (direction == 0) & (element // (CY * EZ) < CX - 1) | (direction == 1) & (element // EZ % CY < CY - 1) | (direction == 2) & (element % EZ < EZ - 1)
        rank_order = jax.random.permutation(key_local, 3 * elements).astype(jnp.int32)
        scores = jnp.where(inner_face, rank_order, rank_order + 3 * elements)
        fixed_face = (candidate == 0) | (candidate == 3 * elements - 2)
        scores = jnp.where(fixed_face, rank_order + 6 * elements, scores)
        chosen = jnp.argsort(scores, stable=True)[:LOC_CAP - 2]
        ends = jnp.array([0, 3 * elements - 2], dtype=jnp.int32)
        return jnp.concatenate([x_ids.astype(jnp.int32), y_ids.astype(jnp.int32), chosen.astype(jnp.int32), ends])
    faces = jax.vmap(one_device)(device_keys)
    return (faces.astype(jnp.int32), counts)


def draw_fracture_faces(key, part):
    return fracture_plan(key)[0]


def draw_fracture_counts(key, part):
    return fracture_plan(key)[1]


def block_scale(own_key, extent, pieces, least, largest):
    def one(position, blocks):
        steps = jax.random.uniform(jax.random.fold_in(jax.random.fold_in(own_key, 6), position), (blocks,), jnp.float32, least / len(pieces), largest / len(pieces))
        return jnp.repeat(jnp.exp(steps), extent[position] // blocks).reshape((-1,) + (1,) * (len(extent) - position - 1))

    gain = one(*pieces[0])
    for cut in pieces[1:]:
        gain = gain * one(*cut)
    return gain


def centred(stream_key, dims, width, limit, cuts=(), held_as=jnp.bfloat16):
    values = jax.random.normal(stream_key, dims, jnp.float32) * width
    if len(cuts) > 0:
        values = block_scale(stream_key, dims, cuts, -0.22, 0.18) * values
    return jnp.clip(values, min=-limit, max=limit).astype(held_as)


def setup_inputs(seed: int = 0) -> dict:
    arg_keys = jax.random.split(jax.random.key(seed), 11)
    displacement = centred(arg_keys[0], (DOF, NX, NY, EZ), 0.5, 4.0, ((1, 8), (2, 4)), jnp.float32)
    velocity = centred(arg_keys[1], (DOF, NX, NY, EZ), 1.0, 6.0, ((1, 8), (2, 4)), jnp.float32)
    modulus = jnp.clip(jnp.exp(math.log(4.0) - 2.0794415 * jax.random.uniform(arg_keys[2], (NX, NY, EZ), jnp.float32) ** block_scale(arg_keys[2], (NX, NY, EZ), ((0, 8), (1, 4)), -0.2, 0.2)), 0.5, 4.0)
    gradient_map = centred(arg_keys[3], (9 * QUAD, DOF), DOF ** -0.5, 0.75, (), jnp.float32)
    trace_map = centred(arg_keys[4], (6, 6 * FACE_QUAD, DOF), DOF ** -0.5, 0.75, (), jnp.float32)
    lift_map = centred(arg_keys[5], (6, DOF, 6 * FACE_QUAD), (6 * 6 * FACE_QUAD) ** -0.5, 0.3125, (), jnp.float32)
    split_map = centred(arg_keys[6], (3 * FACE_QUAD, 3 * FACE_QUAD), (3 * FACE_QUAD) ** -0.5, 1.25, (), jnp.float32)
    spread_map = centred(arg_keys[7], (6, DOF, 3 * FACE_QUAD), (3 * FACE_QUAD) ** -0.5, 1.25, (), jnp.float32)
    fracture_faces = draw_fracture_faces(jax.random.fold_in(arg_keys[10], 71), 0)
    fracture_counts = draw_fracture_counts(jax.random.fold_in(arg_keys[10], 71), 0)
    return dict(displacement=displacement, velocity=velocity, modulus=modulus, gradient_map=gradient_map, trace_map=trace_map, lift_map=lift_map, split_map=split_map, spread_map=spread_map, fracture_faces=fracture_faces, fracture_counts=fracture_counts)


penalty = 2.0
damping = 0.5
substep = 0.1
highest = lax.Precision.HIGHEST


def face_flux(own_traces, own_rates, beside_traces, beside_rates, live_mask):
    value_rows = own_rates.shape[0]
    jump_value = beside_traces[:value_rows] - own_traces[:value_rows]
    upper_rows = penalty * jump_value + 0.5 * (beside_traces[value_rows:] + own_traces[value_rows:]) + damping * (beside_rates - own_rates)
    return jnp.concatenate([upper_rows, 0.5 * jump_value], axis=0) * live_mask


def shift_lower(values):
    return jnp.pad(values[..., :-1], ((0, 0), (0, 0), (0, 0), (1, 0)))


def shift_upper(values):
    return jnp.pad(values[..., 1:], ((0, 0), (0, 0), (0, 0), (0, 1)))


def block_force(slab_displace, slab_velocity, slab_modulus, first_plane, gradient_map, trace_map, lift_map):
    value_rows = trace_map.shape[1] // 2
    traces = jnp.einsum("fkc,cxyz->fkxyz", trace_map, slab_displace, precision=highest)
    rates = jnp.einsum("fkc,cxyz->fkxyz", trace_map[:, :value_rows], slab_velocity, precision=highest)
    centre_traces = traces[:, :, 1:-1, 1:-1]
    centre_rates = rates[:, :, 1:-1, 1:-1]
    beside_traces = [traces[1][:, :-2, 1:-1], traces[0][:, 2:, 1:-1], traces[3][:, 1:-1, :-2], traces[2][:, 1:-1, 2:], shift_lower(centre_traces[5]), shift_upper(centre_traces[4])]
    beside_rates = [rates[1][:, :-2, 1:-1], rates[0][:, 2:, 1:-1], rates[3][:, 1:-1, :-2], rates[2][:, 1:-1, 2:], shift_lower(centre_rates[5]), shift_upper(centre_rates[4])]
    grid_x = (first_plane + jnp.arange(CX, dtype=jnp.int32))[:, None, None]
    grid_y = jnp.arange(NY, dtype=jnp.int32)[None, :, None]
    grid_z = jnp.arange(EZ, dtype=jnp.int32)[None, None, :]
    shape_full = (CX, NY, EZ)
    conditions = (grid_x > 0, grid_x < NX - 1, grid_y > 0, grid_y < NY - 1, grid_z > 0, grid_z < EZ - 1)
    live_masks = [jnp.where(jnp.broadcast_to(condition, shape_full), 1.0, 0.0).astype(jnp.float32) for condition in conditions]
    fluxes = jnp.stack([face_flux(centre_traces[face_index], centre_rates[face_index], beside_traces[face_index], beside_rates[face_index], live_masks[face_index]) for face_index in range(6)])
    lifted = jnp.einsum("fck,fkxyz->cxyz", lift_map, fluxes, precision=highest)
    own_displace = slab_displace[:, 1:-1, 1:-1]
    gradients = jnp.einsum("qc,cxyz->qxyz", gradient_map, own_displace, precision=highest)
    volume = jnp.einsum("qc,qxyz->cxyz", gradient_map, gradients * slab_modulus[None], precision=highest)
    return lifted - volume


def whole_force(displace_now, velocity_now, modulus, gradient_map, trace_map, lift_map):
    padded_displace = jnp.pad(displace_now, ((0, 0), (1, 1), (1, 1), (0, 0)))
    padded_velocity = jnp.pad(velocity_now, ((0, 0), (1, 1), (1, 1), (0, 0)))

    def one_block(block_index):
        first_plane = (block_index * CX).astype(jnp.int32)
        slab_displace = lax.dynamic_slice_in_dim(padded_displace, first_plane, CX + 2, 1)
        slab_velocity = lax.dynamic_slice_in_dim(padded_velocity, first_plane, CX + 2, 1)
        slab_modulus = lax.dynamic_slice_in_dim(modulus, first_plane, CX, 0)
        return block_force(slab_displace, slab_velocity, slab_modulus, first_plane, gradient_map, trace_map, lift_map)

    blocks = lax.map(one_block, jnp.arange(N_PX, dtype=jnp.int32))
    return jnp.moveaxis(blocks, 0, 1).reshape(displace_now.shape)


def open_faces(final_displace, before, fracture_faces, fracture_counts, trace_map, split_map, spread_map):
    devices = N_PX * N_PY
    elements = CX * CY * EZ
    value_rows = 3 * FACE_QUAD
    slots = fracture_faces.shape[1]
    slot_index = jnp.broadcast_to(jnp.arange(slots, dtype=jnp.int32)[None, :], (devices, slots))
    section = jnp.where(slot_index < BLK_CAP, 0, jnp.where(slot_index < 2 * BLK_CAP, 1, 2)).astype(jnp.int32)
    offset = jnp.where(section == 0, 0, jnp.where(section == 1, BLK_CAP, 2 * BLK_CAP)).astype(jnp.int32)
    limits = jnp.take_along_axis(fracture_counts, section, axis=1)
    live_mask = jnp.where(slot_index - offset < limits, 1.0, 0.0).astype(jnp.float32).reshape(-1)
    device = jnp.broadcast_to(jnp.arange(devices, dtype=jnp.int32)[:, None], (devices, slots))
    direction = (fracture_faces // elements).reshape(-1)
    element = fracture_faces % elements
    grid_x = ((device // N_PY) * CX + element // (CY * EZ)).reshape(-1)
    grid_y = ((device % N_PY) * CY + element // EZ % CY).reshape(-1)
    grid_z = (element % EZ).reshape(-1)
    next_x = jnp.minimum(grid_x + (direction == 0).astype(jnp.int32), NX - 1)
    next_y = jnp.minimum(grid_y + (direction == 1).astype(jnp.int32), NY - 1)
    next_z = jnp.minimum(grid_z + (direction == 2).astype(jnp.int32), EZ - 1)
    own_cols = before[:, grid_x, grid_y, grid_z]
    beside_cols = before[:, next_x, next_y, next_z]
    value_map = trace_map[:, :value_rows]
    chooser = [jnp.where(direction == direction_index, 1.0, 0.0).astype(jnp.float32) for direction_index in range(3)]
    own_values = chooser[0] * jnp.dot(value_map[1], own_cols, precision=highest)
    beside_values = chooser[0] * jnp.dot(value_map[0], beside_cols, precision=highest)
    for direction_index in range(1, 3):
        own_values = own_values + chooser[direction_index] * jnp.dot(value_map[2 * direction_index + 1], own_cols, precision=highest)
        beside_values = beside_values + chooser[direction_index] * jnp.dot(value_map[2 * direction_index], beside_cols, precision=highest)
    release = jnp.dot(split_map, beside_values - own_values, precision=highest) * live_mask
    own_push = chooser[0] * jnp.dot(spread_map[1], release, precision=highest)
    beside_push = chooser[0] * jnp.dot(spread_map[0], release, precision=highest)
    for direction_index in range(1, 3):
        own_push = own_push + chooser[direction_index] * jnp.dot(spread_map[2 * direction_index + 1], release, precision=highest)
        beside_push = beside_push + chooser[direction_index] * jnp.dot(spread_map[2 * direction_index], release, precision=highest)
    result = final_displace.at[:, grid_x, grid_y, grid_z].add(-own_push)
    return result.at[:, next_x, next_y, next_z].add(beside_push)


def reference(displacement, velocity, modulus, gradient_map, trace_map, lift_map, split_map, spread_map, fracture_faces, fracture_counts):
    displace_now = displacement
    velocity_now = velocity
    before = displacement
    for subcycle in range(3):
        before = displace_now
        forces = whole_force(displace_now, velocity_now, modulus, gradient_map, trace_map, lift_map)
        velocity_now = velocity_now + substep * forces
        displace_now = displace_now + substep * velocity_now
    opened = open_faces(displace_now, before, fracture_faces, fracture_counts, trace_map, split_map, spread_map)
    return opened, velocity_now
```

```python
import functools

import jax
import jax.numpy as jnp
from jax import lax
from jax.experimental import pallas as pl
from jax.experimental.pallas import tpu as pltpu
from jax.sharding import PartitionSpec as P

BLK_CAP = 128
penalty = 2.0
damping = 0.5
substep = 0.1
F32 = jnp.float32
BF16 = jnp.bfloat16
MESH = pl.DeviceIdType.MESH


def halves(value):
    high = value.astype(BF16)
    return high, (value - high.astype(F32)).astype(BF16)


def mm(a, b):
    return jnp.dot(a, b, preferred_element_type=F32)


def kernel(
    disp, vel, mod, grad, trace, lift, split, spread, faces, counts,
    out_u, out_w,
    state, state_b, wa_h, wa_l, lb_h, lb_hl, ew_hl, tp, gp, lp, pp, qp, proj,
    early_h, early_l, late_h, late_l, jump_h, jump_l, send, recv, send_sem, recv_sem,
):
    px, py = lax.axis_index("px"), lax.axis_index("py")
    nx, ny = lax.axis_size("px"), lax.axis_size("py")
    there = (px > 0, px < nx - 1, py > 0, py < ny - 1)
    beside = ({"px": px - 1}, {"px": px + 1}, {"py": py - 1}, {"py": py + 1})
    barrier = pltpu.get_barrier_semaphore()
    for side in range(4):

        @pl.when(there[side])
        def _(side=side):
            pl.semaphore_signal(barrier, inc=1, device_id=beside[side], device_id_type=MESH)

    state[...] = jnp.zeros_like(state)
    for k in range(4):
        lanes = slice(128 * k, 128 * k + 128)
        state[0:60, lanes] = disp[pl.ds(k, 60, stride=4), :]
        state[64:124, lanes] = vel[pl.ds(k, 60, stride=4), :]

    tp[...] = jnp.zeros_like(tp)
    lp[...] = jnp.zeros_like(lp)
    pp[...] = jnp.zeros_like(pp)
    qp[...] = jnp.zeros_like(qp)
    gp[...] = jnp.zeros_like(gp)
    gp[0:243, 0:60] = grad[...]
    qp[0:27, 0:27] = split[...]
    for f in range(6):
        tp[f, 0:27, 0:60] = trace[f, 0:27, :]
        tp[f, 32:59, 0:60] = trace[f, 27:54, :]
        lp[f, 0:60, 0:54] = lift[f]
        pp[64 * f : 64 * f + 60, 0:27] = spread[f]

    def put_a(row, value):
        high, low = halves(value)
        rows = slice(row, row + value.shape[0])
        wa_h[rows, 0:128] = high
        wa_h[rows, 128:256] = high
        wa_l[rows, :] = low

    for f in range(6):
        tv, tt = tp[f, 0:32, :], tp[f, 32:64, :]
        rate = pltpu.roll(damping * tv, 64, 1)
        put_a(64 * f, penalty * tv + 0.5 * tt + rate)
        put_a(64 * f + 32, tv)
        put_a(384 + 32 * f, penalty * tv - 0.5 * tt + rate)
    put_a(576, gp[...])

    def put_b(column, value):
        high, low = halves(value)
        columns = slice(column, column + value.shape[1])
        lb_h[:, columns] = high
        lb_hl[0:64, columns] = high
        lb_hl[64:128, columns] = low

    lane = lax.broadcasted_iota(jnp.int32, (64, 128), 1)

    def lift_part(f):
        full = lp[f]
        lower = pltpu.roll(jnp.where(lane >= 27, 0.5 * full, 0.0), 5, 1)
        return jnp.where(lane < 27, full, 0.0) + lower

    for d in range(3):
        put_b(128 * d, lift_part(2 * d) + pltpu.roll(lift_part(2 * d + 1), 64, 1))
    put_b(384, -jnp.transpose(gp[...])[0:64, :])
    opened = jnp.dot(pp[...], qp[...], precision=lax.Precision.HIGHEST, preferred_element_type=F32)
    for half in range(2):
        part = jnp.zeros((64, 128), F32)
        for f in range(4 * half, min(6, 4 * half + 4)):
            turned = opened[64 * f : 64 * f + 64]
            part = part + (pltpu.roll(turned, 32 * (f % 4), 1) if f % 4 else turned)
        high, low = halves(-part)
        ew_hl[0:64, 128 * half : 128 * half + 128] = high
        ew_hl[64:128, 128 * half : 128 * half + 128] = low

    jump_h[192:256, :] = jnp.zeros((64, 512), BF16)
    jump_l[192:256, :] = jnp.zeros((64, 512), BF16)

    ids = faces[...]
    slots = lax.broadcasted_iota(jnp.int32, ids.shape, 1)
    limit = jnp.where(
        slots < BLK_CAP,
        counts[0, 0],
        jnp.where(slots < 2 * BLK_CAP, BLK_CAP + counts[0, 1], 2 * BLK_CAP + counts[0, 2]),
    )
    group = jnp.where(slots < limit, ids >> 7, -1)
    spot = ids & 127
    high_hot = lax.broadcasted_iota(jnp.int32, (16, ids.shape[1]), 0) == group
    low_hot = lax.broadcasted_iota(jnp.int32, (128, ids.shape[1]), 0) == spot
    open_mask = lax.dot_general(
        high_hot.astype(F32).astype(BF16),
        low_hot.astype(F32).astype(BF16),
        (((1,), (1,)), ((), ())),
        preferred_element_type=F32,
    )

    for slot, side in ((0, 1), (1, 0), (2, 3), (3, 2)):

        @pl.when(jnp.logical_not(there[side]))
        def _(slot=slot):
            for s in range(3):
                recv[s, slot] = jnp.zeros((64, 256), F32)

    pl.semaphore_wait(barrier, sum(t.astype(jnp.int32) for t in there))

    alive = [jnp.where(t, 1.0, 0.0).astype(F32) for t in there]
    lane_row = lax.broadcasted_iota(jnp.int32, (1, 128), 1)
    not_first = (lane_row > 0).astype(F32)
    not_last = (lane_row < 127).astype(F32)
    copies = [
        [
            pltpu.make_async_remote_copy(
                src_ref=send.at[s, side],
                dst_ref=recv.at[s, side],
                send_sem=send_sem.at[s, side],
                recv_sem=recv_sem.at[s, side],
                device_id=beside[side],
                device_id_type=MESH,
            )
            for side in range(4)
        ]
        for s in range(3)
    ]
    outer = ((0, 1), (2, 3), (0, 2), (1, 3))

    def block(k):
        return slice(128 * k, 128 * k + 128)

    for s in range(3):
        for k in range(4):
            high, low = halves(state[:, block(k)])
            state_b[0:128, block(k)] = high
            state_b[128:256, block(k)] = low
        proj[0:256, :] = mm(wa_h[0:256, :], state_b[...]) + mm(wa_l[0:256, :], state_b[0:128, :])
        for f in range(4):
            for half in range(2):
                k = outer[f][half]
                send[s, f, :, block(half)] = proj[64 * f : 64 * f + 64, block(k)]
                if s == 2 and f % 2 == 1:
                    row = 4 * (f // 2) + k
                    send[s, f, 27:28, block(half)] = open_mask[row : row + 1, :]
        for side in range(4):

            @pl.when(there[side])
            def _(s=s, side=side):
                copies[s][side].start()

        proj[256:832, :] = mm(wa_h[256:832, :], state_b[...]) + mm(
            wa_l[256:832, :], state_b[0:128, :]
        )

        def own(f):
            return 64 * f, 384 + 32 * f

        def difference(f, k, upper, lower):
            at, at_q = own(f)
            return (
                upper - proj[at_q : at_q + 32, block(k)],
                lower - proj[at + 32 : at + 64, block(k)],
            )

        def put(high_ref, low_ref, row, k, value):
            high, low = halves(value)
            rows = slice(row, row + value.shape[0])
            high_ref[rows, block(k)] = high
            low_ref[rows, block(k)] = low

        for k in range(4):
            for f in (4, 5):
                shift, mask = (1, not_first) if f == 4 else (127, not_last)
                other = 64 * (9 - f)
                upper = pltpu.roll(proj[other : other + 32, block(k)], shift, 1)
                lower = pltpu.roll(proj[other + 32 : other + 64, block(k)], shift, 1)
                upper, lower = difference(f, k, upper, lower)
                put(early_h, early_l, 64 * (f - 4), k, upper * mask)
                put(early_h, early_l, 64 * (f - 4) + 32, k, lower * mask)
                if s == 2:
                    opens = open_mask[8 + k : 9 + k, :]
                    if f == 4:
                        opens = pltpu.roll(opens, 1, 1)
                    put(jump_h, jump_l, 32 * f, k, lower * mask * opens)
            put(early_h, early_l, 128, k, proj[576:832, block(k)] * mod[k : k + 1, :])
        both = mm(lb_hl[:, 256:640], early_h[...])
        force = both[0:64] + both[64:128] + mm(lb_h[:, 256:640], early_l[...])

        for side in range(4):

            @pl.when(there[side])
            def _(s=s, side=side):
                copies[s][side ^ 1].wait_recv()

        for k in range(4):
            i, j = k // 2, k % 2
            for f in range(4):
                inner = (i, 1 - i, j, 1 - j)[f] == 1
                n = k ^ (2 if f < 2 else 1)
                if inner:
                    at = 64 * (f ^ 1)
                    upper, lower = proj[at : at + 32, block(n)], proj[at + 32 : at + 64, block(n)]
                else:
                    half = j if f < 2 else i
                    upper, lower = (
                        recv[s, f ^ 1, 0:32, block(half)],
                        recv[s, f ^ 1, 32:64, block(half)],
                    )
                upper, lower = difference(f, k, upper, lower)
                if not inner:
                    upper, lower = upper * alive[f], lower * alive[f]
                put(late_h, late_l, 64 * f, k, upper)
                put(late_h, late_l, 64 * f + 32, k, lower)
                if s == 2:
                    row = 4 * (f // 2)
                    if f % 2:
                        opens = open_mask[row + k : row + k + 1, :]
                    elif inner:
                        opens = open_mask[row + n : row + n + 1, :]
                    else:
                        opens = recv[s, f ^ 1, 27:28, block(half)]
                    put(jump_h, jump_l, 32 * f, k, lower * opens)
        both = mm(lb_hl[:, 0:256], late_h[...])
        force = force + both[0:64] + both[64:128] + mm(lb_h[:, 0:256], late_l[...])
        velocity = state[64:128, :] + substep * force
        displace = state[0:64, :] + substep * velocity
        if s < 2:
            state[64:128, :] = velocity
            state[0:64, :] = displace
        else:
            both = mm(ew_hl[...], jump_h[...])
            displace = displace + both[0:64] + both[64:128] + mm(ew_hl[0:64, :], jump_l[...])
            for k in range(4):
                out_u[pl.ds(k, 60, stride=4), :] = displace[0:60, block(k)]
                out_w[pl.ds(k, 60, stride=4), :] = velocity[0:60, block(k)]

    for s in range(3):
        for side in range(4):

            @pl.when(there[side])
            def _(s=s, side=side):
                copies[s][side].wait_send()


def shards(
    displacement, velocity, modulus, gradient_map, trace_map, lift_map, split_map, spread_map,
    fracture_faces, fracture_counts,
):
    shape = displacement.shape
    components = shape[0]
    flat = (components * 4, 128)
    vmem = pl.BlockSpec(memory_space=pltpu.VMEM)
    smem = pl.BlockSpec(memory_space=pltpu.SMEM)
    out = jax.ShapeDtypeStruct(flat, F32)
    u, w = pl.pallas_call(
        kernel,
        out_shape=(out, out),
        in_specs=[vmem] * 9 + [smem],
        out_specs=(vmem, vmem),
        scratch_shapes=[
            pltpu.VMEM((128, 512), F32),
            pltpu.VMEM((256, 512), BF16),
            pltpu.VMEM((832, 256), BF16),
            pltpu.VMEM((832, 128), BF16),
            pltpu.VMEM((64, 640), BF16),
            pltpu.VMEM((128, 640), BF16),
            pltpu.VMEM((128, 256), BF16),
            pltpu.VMEM((6, 64, 128), F32),
            pltpu.VMEM((256, 128), F32),
            pltpu.VMEM((6, 64, 128), F32),
            pltpu.VMEM((384, 128), F32),
            pltpu.VMEM((128, 128), F32),
            pltpu.VMEM((832, 512), F32),
            pltpu.VMEM((384, 512), BF16),
            pltpu.VMEM((384, 512), BF16),
            pltpu.VMEM((256, 512), BF16),
            pltpu.VMEM((256, 512), BF16),
            pltpu.VMEM((256, 512), BF16),
            pltpu.VMEM((256, 512), BF16),
            pltpu.VMEM((3, 4, 64, 256), F32),
            pltpu.VMEM((3, 4, 64, 256), F32),
            pltpu.SemaphoreType.DMA((3, 4)),
            pltpu.SemaphoreType.DMA((3, 4)),
        ],
        compiler_params=pltpu.CompilerParams(
            collective_id=0, has_side_effects=True, vmem_limit_bytes=40 * 1024 * 1024
        ),
    )(
        displacement.reshape(flat),
        velocity.reshape(flat),
        modulus.reshape(4, 128),
        gradient_map,
        trace_map,
        lift_map,
        split_map,
        spread_map,
        fracture_faces,
        fracture_counts,
    )
    return u.reshape(shape), w.reshape(shape)


def solution(mesh):
    return jax.shard_map(
        shards,
        mesh=mesh,
        in_specs=(
            P(None, "px", "py", None),
            P(None, "px", "py", None),
            P("px", "py", None),
            P(),
            P(),
            P(),
            P(),
            P(),
            P(("px", "py"), None),
            P(("px", "py"), None),
        ),
        out_specs=(P(None, "px", "py", None), P(None, "px", "py", None)),
        check_vma=False,
    )
```

```python
import jax
import jax.numpy as jnp
from jax import lax
from jax.experimental import pallas as pl
from jax.experimental.pallas import tpu as pltpu
from jax.sharding import PartitionSpec as P

BLK_CAP = 128
penalty = 2.0
damping = 0.5
substep = 0.1
F32 = jnp.float32
BF16 = jnp.bfloat16
MESH = pl.DeviceIdType.MESH


def halves(value):
    high = value.astype(BF16)
    return high, (value - high.astype(F32)).astype(BF16)


def mm(a, b):
    return jnp.dot(a, b, preferred_element_type=F32)


def kernel(
    disp_in, vel_in, mod_in, grad_in, trace_in, lift_in, split_in, spread_in, faces_in, counts_in,
    out_u, out_w, out_f,
    disp, vel, mod, grad, trace, lift, split, spread, faces, counts,
    state, state_b, wa_h, wa_l, lb_h, lb_hl, ew_hl, tp, gp, lp, pp, qp, proj,
    early_h, early_l, late_h, late_l, jump_h, jump_l, send, recv, in_sem, send_sem, recv_sem,
):
    px, py = lax.axis_index("px"), lax.axis_index("py")
    nx, ny = lax.axis_size("px"), lax.axis_size("py")
    there = (px > 0, px < nx - 1, py > 0, py < ny - 1)
    beside = ({"px": px - 1}, {"px": px + 1}, {"py": py - 1}, {"py": py + 1})
    barrier = pltpu.get_barrier_semaphore()
    for side in (2, 3, 0, 1):

        @pl.when(there[side])
        def _(side=side):
            pl.semaphore_signal(barrier, inc=1, device_id=beside[side], device_id_type=MESH)

    names = ("trace", "disp", "vel", "grad", "lift", "mod", "spread", "split", "faces", "counts")
    given = (trace_in, disp_in, vel_in, grad_in, lift_in, mod_in, spread_in, split_in, faces_in, counts_in)
    local = (trace, disp, vel, grad, lift, mod, spread, split, faces, counts)
    loads = {}
    for n, name in enumerate(names):
        loads[name] = pltpu.make_async_copy(given[n], local[n], in_sem.at[n])
        loads[name].start()

    for ref in (state, tp, lp, pp, qp, gp):
        ref[...] = jnp.zeros_like(ref)
    for ref in (late_h, late_l, jump_h, jump_l):
        for d in range(ref.shape[0] // 128):
            ref[128 * d + 112 : 128 * d + 128, :] = jnp.zeros((16, 512), BF16)
    for ref in (early_h, early_l):
        ref[112:128, :] = jnp.zeros((16, 512), BF16)
    for slot, side in ((0, 1), (1, 0), (2, 3), (3, 2)):

        @pl.when(jnp.logical_not(there[side]))
        def _(slot=slot):
            for s in range(3):
                recv[s, slot] = jnp.zeros((56, 256), F32)

    def put_a(row, value):
        high, low = halves(value)
        rows = slice(row, row + value.shape[0])
        wa_h[rows, 0:128] = high
        wa_h[rows, 128:256] = high
        wa_l[rows, :] = low

    row_id = lax.broadcasted_iota(jnp.int32, (56, 128), 0)

    def face_rows(f, sign):
        both = tp[f]
        upper = penalty * both + (sign * 0.5) * pltpu.roll(both, 29, 0)
        upper = upper + pltpu.roll(damping * both, 64, 1)
        lower = jnp.where(row_id < 54, pltpu.roll(both, 27, 0), 0.0)
        return jnp.where(row_id < 27, upper, lower)

    def put_faces(row, d, sign):
        pair = [face_rows(2 * d, sign), face_rows(2 * d + 1, sign)]
        put_a(row + 112 * d, jnp.concatenate(pair, axis=0))

    loads["trace"].wait()
    for f in range(6):
        tp[f, 0:54, 0:60] = trace[f]
    put_faces(0, 0, 1.0)
    put_faces(0, 1, 1.0)

    def block(k):
        return slice(128 * k, 128 * k + 128)

    loads["disp"].wait()
    loads["vel"].wait()
    for k in range(4):
        state[0:60, block(k)] = disp[pl.ds(k, 60, stride=4), :]
        state[64:124, block(k)] = vel[pl.ds(k, 60, stride=4), :]

    copies = [
        [
            pltpu.make_async_remote_copy(
                src_ref=send.at[s, side],
                dst_ref=recv.at[s, side],
                send_sem=send_sem.at[s, side],
                recv_sem=recv_sem.at[s, side],
                device_id=beside[side],
                device_id_type=MESH,
            )
            for side in range(4)
        ]
        for s in range(3)
    ]
    outer = ((0, 1), (2, 3), (0, 2), (1, 3))

    def project_outer(s, open_mask=None):
        for k in range(4):
            high, low = halves(state[:, block(k)])
            state_b[0:128, block(k)] = high
            state_b[128:256, block(k)] = low
        for d in (1, 0):
            rows = slice(112 * d, 112 * d + 112)
            proj[rows, :] = mm(wa_h[rows, :], state_b[...]) + mm(wa_l[rows, :], state_b[0:128, :])
            for f in (2 * d, 2 * d + 1):
                for half in range(2):
                    k = outer[f][half]
                    send[s, f, :, block(half)] = proj[56 * f : 56 * f + 56, block(k)]
                    if s == 2 and f % 2 == 1:
                        row = 4 * d + k
                        send[s, f, 54:55, block(half)] = open_mask[row : row + 1, :]
            if s == 0 and d == 1:
                pl.semaphore_wait(barrier, sum(t.astype(jnp.int32) for t in there))
            for side in (2 * d, 2 * d + 1):

                @pl.when(there[side])
                def _(side=side):
                    copies[s][side].start()

    project_outer(0)

    put_faces(0, 2, 1.0)
    for d in range(3):
        put_faces(336, d, -1.0)
    loads["grad"].wait()
    gp[0:60, 0:243] = grad[...]
    put_a(672, jnp.transpose(gp[...]))

    def put_b(column, value):
        high, low = halves(value)
        columns = slice(column, column + value.shape[1])
        lb_h[:, columns] = high
        lb_hl[0:64, columns] = high
        lb_hl[64:128, columns] = low

    put_b(384, -gp[0:64, :])
    loads["lift"].wait()
    lift_row = lax.broadcasted_iota(jnp.int32, (54, 60), 0)
    for f in range(6):
        at = 56 * (f % 2)
        lp[f // 2, at : at + 54, 0:60] = jnp.where(lift_row < 27, lift[f], 0.5 * lift[f])
    for d in range(3):
        put_b(128 * d, jnp.transpose(lp[d])[0:64, :])

    loads["spread"].wait()
    loads["split"].wait()
    qp[0:27, 0:27] = split[...]
    qp[32:59, 0:27] = split[...]
    row128 = lax.broadcasted_iota(jnp.int32, (128, 128), 0)
    placed = jnp.where(row128 < 32, pltpu.roll(qp[...], 27, 1), pltpu.roll(qp[...], 83, 1))
    for f in range(6):
        at = 32 * (f % 2)
        pp[f // 2, at : at + 27, 0:60] = spread[f]
    for d in range(3):
        part = jnp.dot(
            jnp.transpose(pp[d])[0:64, :],
            placed,
            precision=lax.Precision.HIGHEST,
            preferred_element_type=F32,
        )
        high, low = halves(-part)
        ew_hl[0:64, block(d)] = high
        ew_hl[64:128, block(d)] = low

    loads["faces"].wait()
    loads["counts"].wait()
    loads["mod"].wait()
    ids = faces[...]
    slots = lax.broadcasted_iota(jnp.int32, ids.shape, 1)
    section = jnp.where(slots < BLK_CAP, 0, jnp.where(slots < 2 * BLK_CAP, 1, 2))
    limit = jnp.where(
        section == 0,
        counts[0:1, 0:1],
        jnp.where(section == 1, BLK_CAP + counts[0:1, 1:2], 2 * BLK_CAP + counts[0:1, 2:3]),
    )
    group = jnp.where(slots < limit, ids >> 7, -1)
    spot = ids & 127
    high_hot = lax.broadcasted_iota(jnp.int32, (16, ids.shape[1]), 0) == group
    low_hot = lax.broadcasted_iota(jnp.int32, (128, ids.shape[1]), 0) == spot
    open_mask = lax.dot_general(
        high_hot.astype(F32).astype(BF16),
        low_hot.astype(F32).astype(BF16),
        (((1,), (1,)), ((), ())),
        preferred_element_type=F32,
    )

    alive = [jnp.where(t, 1.0, 0.0).astype(F32) for t in there]
    lane_row = lax.broadcasted_iota(jnp.int32, (1, 128), 1)
    not_first = (lane_row > 0).astype(F32)
    not_last = (lane_row < 127).astype(F32)

    def put(high_ref, low_ref, row, k, value):
        high, low = halves(value)
        rows = slice(row, row + value.shape[0])
        high_ref[rows, block(k)] = high
        low_ref[rows, block(k)] = low

    def traced(f, k):
        return proj[56 * f : 56 * f + 56, block(k)]

    def own(f, k):
        return proj[336 + 56 * f : 392 + 56 * f, block(k)]

    for s in range(3):
        if s > 0:
            project_outer(s, open_mask)
        proj[224:928, :] = mm(wa_h[224:928, :], state_b[...]) + mm(
            wa_l[224:928, :], state_b[0:128, :]
        )
        for k in range(4):
            before = (pltpu.roll(traced(5, k), 1, 1) - own(4, k)) * not_first
            after = (pltpu.roll(traced(4, k), 127, 1) - own(5, k)) * not_last
            put(early_h, early_l, 0, k, jnp.concatenate([before, after], axis=0))
            if s == 2:
                opens = open_mask[8 + k : 9 + k, :]
                pair = [before * pltpu.roll(opens, 1, 1), after * opens]
                put(jump_h, jump_l, 256, k, jnp.concatenate(pair, axis=0))
            put(early_h, early_l, 128, k, proj[672:928, block(k)] * mod[k : k + 1, :])
        both = mm(lb_hl[:, 256:640], early_h[...])
        force = both[0:64] + both[64:128] + mm(lb_h[:, 256:640], early_l[...])

        for d in (0, 1):
            for side in (2 * d, 2 * d + 1):

                @pl.when(there[side])
                def _(s=s, side=side):
                    copies[s][side ^ 1].wait_recv()

            for k in range(4):
                i, j = k // 2, k % 2
                n = k ^ (2 if d == 0 else 1)
                half = j if d == 0 else i
                flux, jump = [], []
                for f in (2 * d, 2 * d + 1):
                    inner = (i, 1 - i, j, 1 - j)[f] == 1
                    if inner:
                        part = traced(f ^ 1, n) - own(f, k)
                    else:
                        part = (recv[s, f ^ 1, :, block(half)] - own(f, k)) * alive[f]
                    flux.append(part)
                    if s == 2:
                        if f % 2:
                            opens = open_mask[4 * d + k : 4 * d + k + 1, :]
                        elif inner:
                            opens = open_mask[4 * d + n : 4 * d + n + 1, :]
                        else:
                            opens = recv[s, f ^ 1, 54:55, block(half)]
                        jump.append(part * opens)
                put(late_h, late_l, 128 * d, k, jnp.concatenate(flux, axis=0))
                if s == 2:
                    put(jump_h, jump_l, 128 * d, k, jnp.concatenate(jump, axis=0))
        both = mm(lb_hl[:, 0:256], late_h[...])
        force = force + both[0:64] + both[64:128] + mm(lb_h[:, 0:256], late_l[...])
        if s < 2:
            velocity = state[64:128, :] + substep * force
            state[64:128, :] = velocity
            state[0:64, :] = state[0:64, :] + substep * velocity
        else:
            both = mm(ew_hl[...], jump_h[...])
            displace = state[0:64, :] + both[0:64] + both[64:128] + mm(ew_hl[0:64, :], jump_l[...])
            for k in range(4):
                out_u[pl.ds(k, 60, stride=4), :] = displace[0:60, block(k)]
                out_w[pl.ds(k, 60, stride=4), :] = state[64:124, block(k)]
                out_f[pl.ds(k, 60, stride=4), :] = force[0:60, block(k)]

    for s in range(3):
        for side in range(4):

            @pl.when(there[side])
            def _(s=s, side=side):
                copies[s][side].wait_send()


def shards(
    displacement, velocity, modulus, gradient_map, trace_map, lift_map, split_map, spread_map,
    fracture_faces, fracture_counts,
):
    shape = displacement.shape
    flat = (shape[0] * 4, 128)
    args = (
        displacement.reshape(flat),
        velocity.reshape(flat),
        modulus.reshape(4, 128),
        gradient_map.T,
        trace_map,
        jnp.transpose(lift_map, (0, 2, 1)),
        split_map,
        jnp.transpose(spread_map, (0, 2, 1)),
        fracture_faces,
        fracture_counts,
    )
    vmem = pl.BlockSpec(memory_space=pltpu.VMEM)
    hbm = pl.BlockSpec(memory_space=pltpu.HBM)
    out = jax.ShapeDtypeStruct(flat, F32)
    opened, velocity_now, force = pl.pallas_call(
        kernel,
        out_shape=(out, out, out),
        in_specs=[hbm] * 10,
        out_specs=(vmem, vmem, vmem),
        scratch_shapes=[
            *(pltpu.VMEM(a.shape, a.dtype) for a in args),
            pltpu.VMEM((128, 512), F32),
            pltpu.VMEM((256, 512), BF16),
            pltpu.VMEM((928, 256), BF16),
            pltpu.VMEM((928, 128), BF16),
            pltpu.VMEM((64, 640), BF16),
            pltpu.VMEM((128, 640), BF16),
            pltpu.VMEM((128, 384), BF16),
            pltpu.VMEM((6, 56, 128), F32),
            pltpu.VMEM((128, 256), F32),
            pltpu.VMEM((3, 128, 128), F32),
            pltpu.VMEM((3, 128, 128), F32),
            pltpu.VMEM((128, 128), F32),
            pltpu.VMEM((928, 512), F32),
            pltpu.VMEM((384, 512), BF16),
            pltpu.VMEM((384, 512), BF16),
            pltpu.VMEM((256, 512), BF16),
            pltpu.VMEM((256, 512), BF16),
            pltpu.VMEM((384, 512), BF16),
            pltpu.VMEM((384, 512), BF16),
            pltpu.VMEM((3, 4, 56, 256), F32),
            pltpu.VMEM((3, 4, 56, 256), F32),
            pltpu.SemaphoreType.DMA((10,)),
            pltpu.SemaphoreType.DMA((3, 4)),
            pltpu.SemaphoreType.DMA((3, 4)),
        ],
        compiler_params=pltpu.CompilerParams(
            collective_id=0, has_side_effects=True, vmem_limit_bytes=64 * 1024 * 1024 - 262144
        ),
    )(*args)
    velocity_out = velocity_now + substep * force
    displacement_out = opened + substep * velocity_out
    return displacement_out.reshape(shape), velocity_out.reshape(shape)


def solution(mesh):
    return jax.shard_map(
        shards,
        mesh=mesh,
        in_specs=(
            P(None, "px", "py", None),
            P(None, "px", "py", None),
            P("px", "py", None),
            P(),
            P(),
            P(),
            P(),
            P(),
            P(("px", "py"), None),
            P(("px", "py"), None),
        ),
        out_specs=(P(None, "px", "py", None), P(None, "px", "py", None)),
        check_vma=False,
    )
```

```python
import jax
import jax.numpy as jnp
from jax import lax
from jax.experimental import pallas as pl
from jax.experimental.pallas import tpu as pltpu
from jax.sharding import PartitionSpec as P

BLK_CAP = 128
penalty = 2.0
damping = 0.5
substep = 0.1
F32 = jnp.float32
BF16 = jnp.bfloat16
MESH = pl.DeviceIdType.MESH


def halves(value):
    high = value.astype(BF16)
    return high, (value - high.astype(F32)).astype(BF16)


def mm(a, b):
    return jnp.dot(a, b, preferred_element_type=F32)


def kernel(
    disp_in, vel_in, mod_in, grad_in, trace_in, lift_in, split_in, spread_in, faces_in, counts_in,
    out_u, out_w, out_f,
    disp, vel, mod, grad, trace, lift, split, spread, faces, counts,
    state, state_b, wa_h, wa_l, lb_h, lb_hl, ew_hl, tp, gp, lp, pp, qp, proj,
    early_h, early_l, late_h, late_l, jump_h, jump_l, send, recv, in_sem, send_sem, recv_sem,
):
    px, py = lax.axis_index("px"), lax.axis_index("py")
    nx, ny = lax.axis_size("px"), lax.axis_size("py")
    there = (px > 0, px < nx - 1, py > 0, py < ny - 1)
    beside = ({"px": px - 1}, {"px": px + 1}, {"py": py - 1}, {"py": py + 1})
    barrier = pltpu.get_barrier_semaphore()
    for side in (2, 3, 0, 1):

        @pl.when(there[side])
        def _(side=side):
            pl.semaphore_signal(barrier, inc=1, device_id=beside[side], device_id_type=MESH)

    names = ("trace", "disp", "vel", "grad", "lift", "mod", "spread", "split", "faces", "counts")
    given = (trace_in, disp_in, vel_in, grad_in, lift_in, mod_in, spread_in, split_in, faces_in, counts_in)
    local = (trace, disp, vel, grad, lift, mod, spread, split, faces, counts)
    loads = {}
    for n, name in enumerate(names):
        loads[name] = pltpu.make_async_copy(given[n], local[n], in_sem.at[n])
        loads[name].start()

    for ref in (state, tp, lp, pp, qp, gp):
        ref[...] = jnp.zeros_like(ref)
    for ref in (late_h, late_l, jump_h, jump_l):
        for d in range(ref.shape[0] // 128):
            ref[128 * d + 112 : 128 * d + 128, :] = jnp.zeros((16, 512), BF16)
    for ref in (early_h, early_l):
        ref[112:128, :] = jnp.zeros((16, 512), BF16)
    for slot, side in ((0, 1), (1, 0), (2, 3), (3, 2)):

        @pl.when(jnp.logical_not(there[side]))
        def _(slot=slot):
            for s in range(3):
                recv[s, slot] = jnp.zeros((56, 256), F32)

    def put_a(row, value):
        high, low = halves(value)
        rows = slice(row, row + value.shape[0])
        wa_h[rows, 0:128] = high
        wa_h[rows, 128:256] = high
        wa_l[rows, :] = low

    row_id = lax.broadcasted_iota(jnp.int32, (56, 128), 0)

    def face_rows(f, sign):
        both = tp[f]
        upper = penalty * both + (sign * 0.5) * pltpu.roll(both, 29, 0)
        upper = upper + pltpu.roll(damping * both, 64, 1)
        lower = jnp.where(row_id < 54, pltpu.roll(both, 27, 0), 0.0)
        return jnp.where(row_id < 27, upper, lower)

    def put_faces(row, d, sign):
        pair = [face_rows(2 * d, sign), face_rows(2 * d + 1, sign)]
        put_a(row + 112 * d, jnp.concatenate(pair, axis=0))

    loads["trace"].wait()
    for f in range(6):
        tp[f, 0:54, 0:60] = trace[f]
    put_faces(0, 0, 1.0)
    put_faces(0, 1, 1.0)

    def block(k):
        return slice(128 * k, 128 * k + 128)

    loads["disp"].wait()
    loads["vel"].wait()
    for k in range(4):
        state[0:60, block(k)] = disp[pl.ds(k, 60, stride=4), :]
        state[64:124, block(k)] = vel[pl.ds(k, 60, stride=4), :]

    copies = [
        [
            pltpu.make_async_remote_copy(
                src_ref=send.at[s, side],
                dst_ref=recv.at[s, side],
                send_sem=send_sem.at[s, side],
                recv_sem=recv_sem.at[s, side],
                device_id=beside[side],
                device_id_type=MESH,
            )
            for side in range(4)
        ]
        for s in range(3)
    ]
    outer = ((0, 1), (2, 3), (0, 2), (1, 3))

    def project_outer(s, open_mask=None):
        for k in range(4):
            high, low = halves(state[:, block(k)])
            state_b[0:128, block(k)] = high
            state_b[128:256, block(k)] = low
        for d in (1, 0):
            rows = slice(112 * d, 112 * d + 112)
            proj[rows, :] = mm(wa_h[rows, :], state_b[...]) + mm(wa_l[rows, :], state_b[0:128, :])
            for f in (2 * d, 2 * d + 1):
                for half in range(2):
                    k = outer[f][half]
                    send[s, f, :, block(half)] = proj[56 * f : 56 * f + 56, block(k)]
                    if s == 2 and f % 2 == 1:
                        row = 4 * d + k
                        send[s, f, 54:55, block(half)] = open_mask[row : row + 1, :]
            if s == 0 and d == 1:
                pl.semaphore_wait(barrier, sum(t.astype(jnp.int32) for t in there))
            for side in (2 * d, 2 * d + 1):

                @pl.when(there[side])
                def _(side=side):
                    copies[s][side].start()

    project_outer(0)

    put_faces(0, 2, 1.0)
    for d in range(3):
        put_faces(336, d, -1.0)
    loads["grad"].wait()
    gp[0:60, 0:243] = grad[...]
    put_a(672, jnp.transpose(gp[...]))

    def put_b(column, value):
        high, low = halves(value)
        columns = slice(column, column + value.shape[1])
        lb_h[:, columns] = high
        lb_hl[0:64, columns] = high
        lb_hl[64:128, columns] = low

    put_b(384, -gp[0:64, :])
    loads["lift"].wait()
    lift_row = lax.broadcasted_iota(jnp.int32, (54, 60), 0)
    for f in range(6):
        at = 56 * (f % 2)
        lp[f // 2, at : at + 54, 0:60] = jnp.where(lift_row < 27, lift[f], 0.5 * lift[f])
    for d in range(3):
        put_b(128 * d, jnp.transpose(lp[d])[0:64, :])

    loads["spread"].wait()
    loads["split"].wait()
    qp[0:27, 0:27] = split[...]
    qp[32:59, 0:27] = split[...]
    row128 = lax.broadcasted_iota(jnp.int32, (128, 128), 0)
    placed = jnp.where(row128 < 32, pltpu.roll(qp[...], 27, 1), pltpu.roll(qp[...], 83, 1))
    for f in range(6):
        at = 32 * (f % 2)
        pp[f // 2, at : at + 27, 0:60] = spread[f]
    for d in range(3):
        part = jnp.dot(
            jnp.transpose(pp[d])[0:64, :],
            placed,
            precision=lax.Precision.HIGHEST,
            preferred_element_type=F32,
        )
        high, low = halves(-part)
        ew_hl[0:64, block(d)] = high
        ew_hl[64:128, block(d)] = low

    loads["faces"].wait()
    loads["counts"].wait()
    loads["mod"].wait()
    ids = faces[...]
    slots = lax.broadcasted_iota(jnp.int32, ids.shape, 1)
    section = jnp.where(slots < BLK_CAP, 0, jnp.where(slots < 2 * BLK_CAP, 1, 2))
    limit = jnp.where(
        section == 0,
        counts[0:1, 0:1],
        jnp.where(section == 1, BLK_CAP + counts[0:1, 1:2], 2 * BLK_CAP + counts[0:1, 2:3]),
    )
    group = jnp.where(slots < limit, ids >> 7, -1)
    spot = ids & 127
    high_hot = lax.broadcasted_iota(jnp.int32, (16, ids.shape[1]), 0) == group
    low_hot = lax.broadcasted_iota(jnp.int32, (128, ids.shape[1]), 0) == spot
    open_mask = lax.dot_general(
        high_hot.astype(F32).astype(BF16),
        low_hot.astype(F32).astype(BF16),
        (((1,), (1,)), ((), ())),
        preferred_element_type=F32,
    )

    alive = [jnp.where(t, 1.0, 0.0).astype(F32) for t in there]
    lane_row = lax.broadcasted_iota(jnp.int32, (1, 128), 1)
    not_first = (lane_row > 0).astype(F32)
    not_last = (lane_row < 127).astype(F32)

    def put(high_ref, low_ref, row, k, value):
        high, low = halves(value)
        rows = slice(row, row + value.shape[0])
        high_ref[rows, block(k)] = high
        low_ref[rows, block(k)] = low

    def traced(f, k):
        return proj[56 * f : 56 * f + 56, block(k)]

    def own(f, k):
        return proj[336 + 56 * f : 392 + 56 * f, block(k)]

    for s in range(3):
        if s > 0:
            project_outer(s, open_mask)
        proj[224:928, :] = mm(wa_h[224:928, :], state_b[...]) + mm(
            wa_l[224:928, :], state_b[0:128, :]
        )
        for k in range(4):
            before = (pltpu.roll(traced(5, k), 1, 1) - own(4, k)) * not_first
            after = (pltpu.roll(traced(4, k), 127, 1) - own(5, k)) * not_last
            put(early_h, early_l, 0, k, jnp.concatenate([before, after], axis=0))
            if s == 2:
                opens = open_mask[8 + k : 9 + k, :]
                pair = [before * pltpu.roll(opens, 1, 1), after * opens]
                put(jump_h, jump_l, 256, k, jnp.concatenate(pair, axis=0))
            put(early_h, early_l, 128, k, proj[672:928, block(k)] * mod[k : k + 1, :])
        both = mm(lb_hl[:, 256:640], early_h[...])
        force = both[0:64] + both[64:128] + mm(lb_h[:, 256:640], early_l[...])

        for d in (0, 1):
            for side in (2 * d, 2 * d + 1):

                @pl.when(there[side])
                def _(s=s, side=side):
                    copies[s][side ^ 1].wait_recv()

            for k in range(4):
                i, j = k // 2, k % 2
                n = k ^ (2 if d == 0 else 1)
                half = j if d == 0 else i
                flux, jump = [], []
                for f in (2 * d, 2 * d + 1):
                    inner = (i, 1 - i, j, 1 - j)[f] == 1
                    if inner:
                        part = traced(f ^ 1, n) - own(f, k)
                    else:
                        part = (recv[s, f ^ 1, :, block(half)] - own(f, k)) * alive[f]
                    flux.append(part)
                    if s == 2:
                        if f % 2:
                            opens = open_mask[4 * d + k : 4 * d + k + 1, :]
                        elif inner:
                            opens = open_mask[4 * d + n : 4 * d + n + 1, :]
                        else:
                            opens = recv[s, f ^ 1, 54:55, block(half)]
                        jump.append(part * opens)
                put(late_h, late_l, 128 * d, k, jnp.concatenate(flux, axis=0))
                if s == 2:
                    put(jump_h, jump_l, 128 * d, k, jnp.concatenate(jump, axis=0))
        both = mm(lb_hl[:, 0:256], late_h[...])
        force = force + both[0:64] + both[64:128] + mm(lb_h[:, 0:256], late_l[...])
        if s < 2:
            velocity = state[64:128, :] + substep * force
            state[64:128, :] = velocity
            state[0:64, :] = state[0:64, :] + substep * velocity
        else:
            both = mm(ew_hl[...], jump_h[...])
            displace = state[0:64, :] + both[0:64] + both[64:128] + mm(ew_hl[0:64, :], jump_l[...])
            for k in range(4):
                out_u[pl.ds(k, 60, stride=4), :] = displace[0:60, block(k)]
                out_w[pl.ds(k, 60, stride=4), :] = state[64:124, block(k)]
                out_f[pl.ds(k, 60, stride=4), :] = force[0:60, block(k)]

    for s in range(3):
        for side in range(4):

            @pl.when(there[side])
            def _(s=s, side=side):
                copies[s][side].wait_send()


def shards(
    displacement, velocity, modulus, gradient_map, trace_map, lift_map, split_map, spread_map,
    fracture_faces, fracture_counts,
):
    shape = displacement.shape
    flat = (shape[0] * 4, 128)
    args = (
        displacement.reshape(flat),
        velocity.reshape(flat),
        modulus.reshape(4, 128),
        gradient_map.T,
        trace_map,
        jnp.transpose(lift_map, (0, 2, 1)),
        split_map,
        jnp.transpose(spread_map, (0, 2, 1)),
        fracture_faces,
        fracture_counts,
    )
    vmem = pl.BlockSpec(memory_space=pltpu.VMEM)
    hbm = pl.BlockSpec(memory_space=pltpu.HBM)
    out = jax.ShapeDtypeStruct(flat, F32)
    opened, velocity_now, force = pl.pallas_call(
        kernel,
        out_shape=(out, out, out),
        in_specs=[hbm] * 10,
        out_specs=(vmem, vmem, vmem),
        scratch_shapes=[
            *(pltpu.VMEM(a.shape, a.dtype) for a in args),
            pltpu.VMEM((128, 512), F32),
            pltpu.VMEM((256, 512), BF16),
            pltpu.VMEM((928, 256), BF16),
            pltpu.VMEM((928, 128), BF16),
            pltpu.VMEM((64, 640), BF16),
            pltpu.VMEM((128, 640), BF16),
            pltpu.VMEM((128, 384), BF16),
            pltpu.VMEM((6, 56, 128), F32),
            pltpu.VMEM((128, 256), F32),
            pltpu.VMEM((3, 128, 128), F32),
            pltpu.VMEM((3, 128, 128), F32),
            pltpu.VMEM((128, 128), F32),
            pltpu.VMEM((928, 512), F32),
            pltpu.VMEM((384, 512), BF16),
            pltpu.VMEM((384, 512), BF16),
            pltpu.VMEM((256, 512), BF16),
            pltpu.VMEM((256, 512), BF16),
            pltpu.VMEM((384, 512), BF16),
            pltpu.VMEM((384, 512), BF16),
            pltpu.VMEM((3, 4, 56, 256), F32),
            pltpu.VMEM((3, 4, 56, 256), F32),
            pltpu.SemaphoreType.DMA((10,)),
            pltpu.SemaphoreType.DMA((3, 4)),
            pltpu.SemaphoreType.DMA((3, 4)),
        ],
        compiler_params=pltpu.CompilerParams(
            collective_id=0, has_side_effects=True, vmem_limit_bytes=40 * 1024 * 1024
        ),
    )(*(pltpu.with_memory_space_constraint(a, pltpu.HBM) for a in args))
    velocity_out = velocity_now + substep * force
    displacement_out = opened + substep * velocity_out
    return displacement_out.reshape(shape), velocity_out.reshape(shape)


def solution(mesh):
    return jax.shard_map(
        shards,
        mesh=mesh,
        in_specs=(
            P(None, "px", "py", None),
            P(None, "px", "py", None),
            P("px", "py", None),
            P(),
            P(),
            P(),
            P(),
            P(),
            P(("px", "py"), None),
            P(("px", "py"), None),
        ),
        out_specs=(P(None, "px", "py", None), P(None, "px", "py", None)),
        check_vma=False,
    )
```
